32 devices in a mesh: gx: 4 (over y, core), gy: 8 (over z, x).
Axes of the slice: x: 2, y: 2, z: 4, core: 2. Of those that a mesh axis runs over, the one named last changes fastest.
Arguments:
- dens_pres: float32 [2, 32, 128, 128], P(None, 'gx', 'gy'), may hold values from 0.7 to 1.3
- velocity: float32 [3, 32, 128, 128], P(None, 'gx', 'gy'), may hold values from -0.9 to 0.9
- cut_class: int32 [32, 128, 128], P('gx', 'gy'), may hold values from 0 to 3
- nbhd_cells: int32 [4, 8, 32, 64], P('gx', 'gy'), may hold values from 0 to 16383, as said below
- helper_list: int32 [4, 8, 32], P('gx', 'gy'), may hold values from 0 to 7, as said below
- live_counts: int32 [4, 8], P('gx', 'gy'), may hold values from 16 to 32, as said below
- redist_weights: float32 [4, 8, 8, 8, 64, 64], P('gx', 'gy'), may hold values from -0.2 to 0.7
Outputs:
- new_state: float32 [5, 32, 128, 128], P(None, 'gx', 'gy')
The draws below stay inside these ranges and needn't reach their ends.
Inputs may be any that keep to these rules, and one draw needn't show every extreme that they name: `nbhd_cells`: in each grid block the 32 x 64 entries are distinct cell numbers of that block. `helper_list`: in each grid block no helper is named by more than 8 slots, and at least one helper is named by exactly 8. `live_counts`: the slots below the count are live.
All inputs are finite; a program needn't handle non-finite values.
Results may differ from the reference program's by a relative error of at most 0.0003.
Values sent between devices are 32-bit elements; how exact they have to be, the bound alone decides.
A program may use at most 64 MiB of HBM per device.

```python
import jax
import jax.numpy as jnp
from jax import lax

CX = 8
CY = 16
NZ = 128
NBR = 64
NB_DEV = 32
CAP = 8
NX = 32
NY = 128
N_GX = 4
N_GY = 8


def draw_nbhd_cells(key, part):
    keys = jax.random.split(key, N_GX * N_GY)

    def single(subkey):
        order = jax.random.permutation(subkey, CX * CY * NZ)
        return order[:NB_DEV * NBR].reshape(NB_DEV, NBR).astype(jnp.int32)
    return jax.vmap(single)(keys).reshape(N_GX, N_GY, NB_DEV, NBR)


def draw_helper_list(key, part):
    keys = jax.random.split(key, N_GX * N_GY)
    base_pool = jnp.repeat(jnp.arange(N_GY, dtype=jnp.int32), CAP)

    def single(subkey):
        first_key, second_key, third_key = jax.random.split(subkey, 3)
        leader = jax.random.randint(first_key, (), 0, N_GY)
        rolled = jnp.roll(base_pool, -leader * CAP)
        others = jax.random.permutation(second_key, rolled[CAP:])
        listed = jnp.concatenate([rolled[:CAP], others])[:NB_DEV]
        return jax.random.permutation(third_key, listed).astype(jnp.int32)
    return jax.vmap(single)(keys).reshape(N_GX, N_GY, NB_DEV)


def draw_live_counts(key, part):
    total = N_GX * N_GY
    first_key, second_key, third_key = jax.random.split(key, 3)
    counts = jax.random.randint(first_key, (total,), NB_DEV // 2, NB_DEV + 1)
    fullest = jax.random.randint(second_key, (), 0, total)
    emptiest = (fullest + 1 + jax.random.randint(third_key, (), 0, total - 1)) % total
    counts = counts.at[fullest].set(NB_DEV).at[emptiest].set(NB_DEV // 2)
    return counts.reshape(N_GX, N_GY).astype(jnp.int32)


def draw_redist_weights(key, part):
    shape = (N_GX, N_GY, N_GY, CAP, NBR, NBR)
    spread = jnp.clip(jax.random.normal(key, shape, jnp.float32), -4.0, 4.0) * 0.05
    rows = lax.broadcasted_iota(jnp.int32, shape, 4)
    columns = lax.broadcasted_iota(jnp.int32, shape, 5)
    return spread + jnp.where(rows == columns, 0.5, 0.0).astype(jnp.float32)


def set_ends(result, stream_key, smallest, largest):
    place = [jax.random.randint(jax.random.fold_in(stream_key, axis), (), 0, length) for axis, length in enumerate(result.shape)]
    longest = result.shape.index(max(result.shape))
    next_to = place[:longest] + [(place[longest] + 1) % result.shape[longest]] + place[longest + 1:]
    return result.at[tuple(place)].set(smallest).at[tuple(next_to)].set(largest)


def shard_levels(key, extent, shards, least, top_value):
    factor_of, own = 1.0, jax.random.fold_in(key, 6)
    for position, shards_of in shards:
        heights = jnp.exp(jax.random.uniform(jax.random.fold_in(own, position), (shards_of,), jnp.float32, least / len(shards), top_value / len(shards)))
        factor_of = factor_of * jnp.repeat(heights, extent[position] // shards_of).reshape([-1 if axis == position else 1 for axis in range(len(extent))])
    return factor_of


def gaussian(stream_key, extent, scale, most, shards=(), kind=jnp.bfloat16):
    factor_of = shard_levels(stream_key, extent, shards, -0.22, 0.18) if shards else 1.0
    drawn = jax.random.normal(stream_key, extent, jnp.float32) * scale * factor_of
    return jnp.minimum(jnp.maximum(drawn, -most), most).astype(kind)


def setup_inputs(seed: int = 0) -> dict:
    streams_of = jax.random.split(jax.random.key(seed), 8)
    dens_pres = jnp.clip(0.7 + 0.59999996 * jax.random.uniform(streams_of[0], (2, NX, NY, NZ), jnp.float32) ** shard_levels(streams_of[0], (2, NX, NY, NZ), ((1, 4), (2, 8)), -0.2, 0.2), 0.7, 1.3)
    velocity = gaussian(streams_of[1], (3, NX, NY, NZ), 0.3, 0.9, ((1, 4), (2, 8)), jnp.float32)
    cut_class = set_ends(jax.random.randint(streams_of[2], (NX, NY, NZ), 0, 4), jax.random.fold_in(streams_of[2], 1), 0, 3).astype(jnp.int32)
    nbhd_cells = draw_nbhd_cells(jax.random.fold_in(streams_of[7], 71), 0)
    helper_list = draw_helper_list(jax.random.fold_in(streams_of[7], 71), 0)
    live_counts = draw_live_counts(jax.random.fold_in(streams_of[7], 71), 0)
    redist_weights = draw_redist_weights(jax.random.fold_in(streams_of[7], 71), 0)
    return {"dens_pres": dens_pres, "velocity": velocity, "cut_class": cut_class, "nbhd_cells": nbhd_cells, "helper_list": helper_list, "live_counts": live_counts, "redist_weights": redist_weights}


GAS_GAMMA = 1.4
STEP_RATIO = 0.3

def minmod(lower_diff, upper_diff):
    return 0.5 * (jnp.sign(lower_diff) + jnp.sign(upper_diff)) * jnp.minimum(jnp.abs(lower_diff), jnp.abs(upper_diff))

def conserved(primitive):
    density = primitive[0]
    speeds = primitive[1:4]
    pressure = primitive[4]
    energy = pressure / (GAS_GAMMA - 1.0) + 0.5 * density * lax.optimization_barrier(jnp.sum(speeds * speeds, axis=0))
    return jnp.concatenate([density[None], density[None] * speeds, energy[None]], axis=0)

def face_flux(primitive, normal):
    density = primitive[0]
    pressure = primitive[4]
    normal_speed = primitive[1 + normal]
    state = conserved(primitive)
    flux = state * normal_speed[None]
    flux = flux.at[1 + normal].add(pressure)
    flux = flux.at[4].add(pressure * normal_speed)
    sound = jnp.sqrt(GAS_GAMMA * pressure / density)
    return (state, flux, jnp.abs(normal_speed) + sound)

def rusanov(lower_state, upper_state, normal):
    cons_low, flux_low, speed_low = face_flux(lower_state, normal)
    cons_up, flux_up, speed_up = face_flux(upper_state, normal)
    wave = jnp.maximum(speed_low, speed_up)
    return 0.5 * (flux_low + flux_up) - 0.5 * wave[None] * (cons_up - cons_low)

def piece(array, start, stop, axis):
    return lax.slice_in_dim(array, start, stop, axis=axis)

def divergence(padded, normal):
    axis = normal + 1
    length = padded.shape[axis] - 4
    jumps = piece(padded, 1, length + 4, axis) - piece(padded, 0, length + 3, axis)
    slopes = minmod(piece(jumps, 0, length + 2, axis), piece(jumps, 1, length + 3, axis))
    centres = piece(padded, 1, length + 3, axis)
    lower_state = piece(centres, 0, length + 1, axis) + 0.5 * piece(slopes, 0, length + 1, axis)
    upper_state = piece(centres, 1, length + 2, axis) - 0.5 * piece(slopes, 1, length + 2, axis)
    fluxes = rusanov(lower_state, upper_state, normal)
    return piece(fluxes, 1, length + 1, axis) - piece(fluxes, 0, length, axis)

def wrap_pad(array, axis):
    widths = [(0, 0)] * array.ndim
    widths[axis] = (2, 2)
    return jnp.pad(array, widths, mode='wrap')

def slot_ranks(helper_row):
    count = helper_row.shape[0]
    same = helper_row[None, :] == helper_row[:, None]
    lower = lax.broadcasted_iota(jnp.int32, (count, count), 1) < lax.broadcasted_iota(jnp.int32, (count, count), 0)
    return lax.optimization_barrier(jnp.sum((same & lower).astype(jnp.int32), axis=1)).astype(jnp.int32)

def reference(dens_pres, velocity, cut_class, nbhd_cells, helper_list, live_counts, redist_weights):
    primitive = jnp.concatenate([dens_pres[0:1], velocity, dens_pres[1:2]], axis=0)
    total_div = divergence(wrap_pad(primitive, 1), 0)
    total_div = total_div + divergence(wrap_pad(primitive, 2), 1)
    total_div = total_div + divergence(wrap_pad(primitive, 3), 2)
    kappa = 0.25 * (1.0 + cut_class.astype(jnp.float32))
    delta = -STEP_RATIO * total_div / kappa[None]
    blocks = delta.reshape(5, N_GX, CX, N_GY, CY, NZ).transpose(1, 3, 0, 2, 4, 5).reshape(N_GX, N_GY, 5, CX * CY * NZ)
    column_ids = jnp.arange(N_GY, dtype=jnp.int32)

    def per_group(inputs):
        block_row, cell_row, helper_row, count_row, weight_row = inputs

        def per_block(block, cells, helpers, count, column):
            ranks = slot_ranks(helpers)
            values = block[:, cells]
            chosen = weight_row[helpers, column, ranks]
            mixed = jnp.einsum('nij,vnj->vni', chosen, values, precision=lax.Precision.HIGHEST)
            live = jnp.arange(NB_DEV, dtype=jnp.int32) < count
            mixed = jnp.where(live[None, :, None], mixed, values)
            return block.at[:, cells.reshape(-1)].set(mixed.reshape(5, -1))
        return jax.vmap(per_block)(block_row, cell_row, helper_row, count_row, column_ids)
    blocks = lax.map(per_group, (blocks, nbhd_cells, helper_list, live_counts, redist_weights))
    delta = blocks.reshape(N_GX, N_GY, 5, CX, CY, NZ).transpose(2, 0, 3, 1, 4, 5).reshape(5, N_GX * CX, N_GY * CY, NZ)
    return conserved(primitive) + delta
```

```python
import functools

import jax
import jax.numpy as jnp
from jax import lax
from jax.experimental import pallas as pl
from jax.experimental.pallas import tpu as pltpu
from jax.sharding import PartitionSpec as P

GAS_GAMMA = 1.4
STEP_RATIO = 0.3
MESH = pl.DeviceIdType.MESH
NT = (((1,), (1,)), ((), ()))
LANES = 128


def minmod(a, b):
    return jnp.maximum(jnp.minimum(a, b), 0.0) + jnp.minimum(jnp.maximum(a, b), 0.0)


def conserved(q):
    rho, u, v, w, p = q
    energy = p * (1.0 / (GAS_GAMMA - 1.0)) + 0.5 * rho * (u * u + v * v + w * w)
    return [rho, rho * u, rho * v, rho * w, energy]


def state_flux(q, normal):
    rho, p, un = q[0], q[4], q[1 + normal]
    cons = conserved(q)
    flux = [part * un for part in cons]
    flux[1 + normal] = flux[1 + normal] + p
    flux[4] = flux[4] + p * un
    gp = GAS_GAMMA * p
    return cons, flux, jnp.abs(un) + gp * lax.rsqrt(gp * rho)


def double_flux(lower, upper, normal):
    cl, fl, sl = state_flux(lower, normal)
    cu, fu, su = state_flux(upper, normal)
    wave = jnp.maximum(sl, su)
    return [a + b - wave * (d - c) for a, b, c, d in zip(fl, fu, cl, cu)]


def cyclic_divergence(q, normal, axis):
    size = q[0].shape[axis]
    before = lambda t: pltpu.roll(t, 1, axis)
    after = lambda t: pltpu.roll(t, size - 1, axis)
    jumps = [t - before(t) for t in q]
    halves = [0.5 * minmod(j, after(j)) for j in jumps]
    lower = [t + s for t, s in zip(q, halves)]
    upper = [after(t - s) for t, s in zip(q, halves)]
    flux = double_flux(lower, upper, normal)
    return [f - before(f) for f in flux]


def split2(t):
    high = t.astype(jnp.bfloat16)
    return high, (t - high.astype(jnp.float32)).astype(jnp.bfloat16)


def kernel(ngx, ngy, dp_ref, vel_ref, cut_ref, cells_ref, help_ref, live_ref, w_ref, out_ref,
           px, py, ysend, yrecv, cutv, wv, acc, dmat, ridx, zidx, ohr, ohz, wbd,
           sendv, arrived, mixed, returned,
           lsem, hsend, hrecv, asend, arecv, bsend, brecv):
    gx = lax.axis_index("gx")
    gy = lax.axis_index("gy")
    _, cx, cy, nz = dp_ref.shape
    cap, nbr = w_ref.shape[3], w_ref.shape[4]
    slots = cells_ref.shape[2]
    pack = LANES // nbr
    rows = cap // pack
    entries = cap * nbr
    cells_xy = cx * cy

    loads = [
        pltpu.make_async_copy(dp_ref.at[0], px.at[0, pl.ds(2, cx)], lsem.at[0]),
        pltpu.make_async_copy(dp_ref.at[1], px.at[4, pl.ds(2, cx)], lsem.at[1]),
        pltpu.make_async_copy(vel_ref, px.at[pl.ds(1, 3), pl.ds(2, cx)], lsem.at[2]),
    ]
    later = [
        pltpu.make_async_copy(w_ref.at[0, 0], wv, lsem.at[3]),
        pltpu.make_async_copy(cut_ref, cutv, lsem.at[4]),
    ]
    for copy in loads + later:
        copy.start()

    xlo = {"gx": lax.rem(gx + ngx - 1, ngx)}
    xhi = {"gx": lax.rem(gx + 1, ngx)}
    ylo = {"gy": lax.rem(gy + ngy - 1, ngy)}
    yhi = {"gy": lax.rem(gy + 1, ngy)}
    barrier = pltpu.get_barrier_semaphore()
    for target in (xlo, xhi):
        pl.semaphore_signal(barrier, inc=1, device_id=target, device_id_type=MESH)
    for k in range(1, ngy):
        pl.semaphore_signal(barrier, inc=1, device_id={"gy": lax.rem(gy + k, ngy)}, device_id_type=MESH)

    for copy in loads:
        copy.wait()

    def fill_rows(x, carry):
        for v in range(5):
            q = px[v, x + 2]
            py[v, x, pl.ds(0, cy), :] = q
            ysend[0, v, x] = q[0:2]
            ysend[1, v, x] = q[cy - 2:cy]
        return carry

    lax.fori_loop(0, cx, fill_rows, 0)
    pl.semaphore_wait(barrier, ngy + 1)

    def remote(src, dst, send, recv, target):
        return pltpu.make_async_remote_copy(src_ref=src, dst_ref=dst, send_sem=send, recv_sem=recv,
                                            device_id=target, device_id_type=MESH)

    halos = [
        remote(px.at[:, pl.ds(2, 2)], px.at[:, pl.ds(cx + 2, 2)], hsend.at[0], hrecv.at[0], xlo),
        remote(px.at[:, pl.ds(cx, 2)], px.at[:, pl.ds(0, 2)], hsend.at[1], hrecv.at[1], xhi),
        remote(ysend.at[0], yrecv.at[1], hsend.at[2], hrecv.at[2], ylo),
        remote(ysend.at[1], yrecv.at[0], hsend.at[3], hrecv.at[3], yhi),
    ]
    for copy in halos:
        copy.start()

    names = help_ref[0].astype(jnp.float32)
    sub = lax.broadcasted_iota(jnp.int32, (slots, slots), 0)
    lane = lax.broadcasted_iota(jnp.int32, (slots, slots), 1)
    spread = jnp.broadcast_to(names, (slots, slots))
    column = jnp.sum(jnp.where(sub == lane, spread, 0.0), axis=1, keepdims=True)
    ranks = jnp.sum(jnp.where((column == spread) & (sub < lane), 1.0, 0.0), axis=0, keepdims=True)
    place = names * float(cap) + ranks
    live = lax.broadcasted_iota(jnp.int32, (1, slots), 1) < live_ref[...]
    place = jnp.where(live, place, -1.0)
    cells = cells_ref[0, 0]
    shift = nz.bit_length() - 1
    cell_row = ((cells >> shift) + 1).astype(jnp.float32).astype(jnp.bfloat16)
    cell_z = ((cells & (nz - 1)) + 1).astype(jnp.float32).astype(jnp.bfloat16)
    total = ngy * rows
    target_row = lax.broadcasted_iota(jnp.int32, (total, slots), 0) * pack
    parts_r, parts_z = [], []
    for j in range(pack):
        hot = jnp.where((target_row + j).astype(jnp.float32) == place, 1.0, 0.0).astype(jnp.bfloat16)
        parts_r.append(jnp.dot(hot, cell_row, preferred_element_type=jnp.float32))
        parts_z.append(jnp.dot(hot, cell_z, preferred_element_type=jnp.float32))
    ridx[...] = jnp.concatenate(parts_r, axis=1).astype(jnp.int32) - 1
    zidx[...] = jnp.concatenate(parts_z, axis=1).astype(jnp.int32) - 1

    def lane_row(ref, h):
        return jnp.concatenate([ref[pl.ds(h * rows + i, 1), :] for i in range(rows)], axis=1)

    def one_hots(h, carry):
        r_of = lane_row(ridx, h)
        z_of = lane_row(zidx, h)
        ohr[h] = jnp.where(lax.broadcasted_iota(jnp.int32, (cells_xy, entries), 0) == r_of, 1.0, 0.0).astype(jnp.bfloat16)
        ohz[h] = jnp.where(lax.broadcasted_iota(jnp.int32, (nz, entries), 0) == z_of, 1.0, 0.0).astype(jnp.bfloat16)
        return carry

    lax.fori_loop(0, ngy, one_hots, 0)

    def z_part(x, carry):
        for v, t in enumerate(cyclic_divergence([px[v, x + 2] for v in range(5)], 2, 1)):
            acc[v, x + 1] = t
        return carry

    lax.fori_loop(0, cx, z_part, 0)

    for copy in later:
        copy.wait()

    def weights(t, carry):
        b = t // rows
        i = t % rows
        for part in range(2):
            for j in range(pack):
                high, low = split2(wv[b, i * pack + j])
                piece = high if part == 0 else low
                blank = jnp.zeros((nbr, nbr), jnp.bfloat16)
                full = jnp.concatenate([blank] * j + [piece] + [blank] * (pack - 1 - j), axis=1)
                wbd[t, pl.ds(part * LANES + j * nbr, nbr), :] = full
        return carry

    lax.fori_loop(0, total, weights, 0)

    halos[0].wait_recv()
    halos[1].wait_recv()

    jump0 = [px[v, 1] - px[v, 0] for v in range(5)]
    jump1 = [px[v, 2] - px[v, 1] for v in range(5)]
    low0 = [px[v, 1] + 0.5 * minmod(jump0[v], jump1[v]) for v in range(5)]

    def x_part(f, carry):
        lower, jump, before = carry
        here = [px[v, f + 2] for v in range(5)]
        ahead = [px[v, f + 3] - here[v] for v in range(5)]
        halves = [0.5 * minmod(a, b) for a, b in zip(jump, ahead)]
        flux = double_flux(lower, [t - s for t, s in zip(here, halves)], 0)
        for v in range(5):
            acc[v, f] += flux[v] - before[v]
        return [t + s for t, s in zip(here, halves)], ahead, flux

    for v in range(5):
        acc[v, 0] = jnp.zeros((cy, nz), jnp.float32)
    lax.fori_loop(0, cx + 1, x_part, (low0, jump1, [jnp.zeros((cy, nz), jnp.float32)] * 5))

    halos[2].wait_recv()
    halos[3].wait_recv()

    def y_part(x, carry):
        for v in range(5):
            py[v, x, pl.ds(cy, 2), :] = yrecv[1, v, x]
            py[v, x, pl.ds(cy + 2, 2), :] = yrecv[1, v, x]
            py[v, x, pl.ds(cy + 4, 2), :] = yrecv[0, v, x]
            py[v, x, pl.ds(cy + 6, 2), :] = yrecv[0, v, x]
        q = [py[v, x] for v in range(5)]
        div = cyclic_divergence(q, 1, 0)
        scale = (-2.0 * STEP_RATIO) / (1.0 + cutv[x].astype(jnp.float32))
        cons = conserved([t[0:cy] for t in q])
        for v in range(5):
            delta = (acc[v, x + 1] + div[v][0:cy]) * scale
            out_ref[v, x] = cons[v] + delta
            high, low = split2(delta)
            start = pl.multiple_of(x * cy, cy)
            dmat[v, pl.ds(start, cy), pl.ds(0, nz)] = high
            dmat[v, pl.ds(start, cy), pl.ds(nz, nz)] = low
        return carry

    lax.fori_loop(0, cx, y_part, 0)

    def gather(k, h):
        hot_z = ohz[h]
        stacked = jnp.concatenate([hot_z, hot_z], axis=0)
        mask = lax.broadcasted_iota(jnp.int32, (cells_xy, entries), 0) == lane_row(ridx, h)
        for v in range(5):
            picked = jnp.dot(dmat[v], stacked, preferred_element_type=jnp.float32)
            sendv[k, pl.ds(v, 1), :] = jnp.sum(jnp.where(mask, picked, 0.0), axis=0, keepdims=True)

    def mix(source, k, dest):
        b = lax.rem(gy + ngy - k, ngy)
        for i in range(rows):
            high, low = split2(source[k, :, pl.ds(i * LANES, LANES)])
            w = wbd[b * rows + i]
            first = lax.dot_general(high, w, NT, preferred_element_type=jnp.float32)
            second = lax.dot_general(low, w[0:LANES], NT, preferred_element_type=jnp.float32)
            dest[k, :, pl.ds(i * LANES, LANES)] = first[:, 0:LANES] + first[:, LANES:] + second

    def scatter(k):
        h = lax.rem(gy + k, ngy)
        high, low = split2(returned[k] - sendv[k])
        hot_r = ohr[h]
        hot_z = ohz[h]
        for v in range(5):
            moved = lax.dot_general(hot_r * high[v:v + 1], hot_z, NT, preferred_element_type=jnp.float32)
            moved += lax.dot_general(hot_r * low[v:v + 1], hot_z, NT, preferred_element_type=jnp.float32)
            out_ref[v] += moved.reshape(cx, cy, nz)

    out_copies, back_copies = [None], [None]
    for k in range(1, ngy):
        target = {"gy": lax.rem(gy + k, ngy)}
        gather(k, lax.rem(gy + k, ngy))
        copy = remote(sendv.at[k], arrived.at[k], asend.at[k], arecv.at[k], target)
        copy.start()
        out_copies.append(copy)
    gather(0, gy)
    mix(sendv, 0, returned)
    for k in range(1, ngy):
        out_copies[k].wait_recv()
        mix(arrived, k, mixed)
        source = {"gy": lax.rem(gy + ngy - k, ngy)}
        copy = remote(mixed.at[k], returned.at[k], bsend.at[k], brecv.at[k], source)
        copy.start()
        back_copies.append(copy)
    scatter(0)
    for k in range(1, ngy):
        back_copies[k].wait_recv()
        scatter(k)
    for copy in halos + out_copies[1:] + back_copies[1:]:
        copy.wait_send()


def local(ngx, ngy, dens_pres, velocity, cut_class, nbhd_cells, helper_list, live_counts, redist_weights):
    _, cx, cy, nz = dens_pres.shape
    cap, nbr = redist_weights.shape[3:5]
    pack = LANES // nbr
    rows = cap // pack
    total = ngy * rows
    entries = cap * nbr
    f32, bf16 = jnp.float32, jnp.bfloat16
    hbm = pl.BlockSpec(memory_space=pl.ANY)
    vmem = pl.BlockSpec(memory_space=pltpu.VMEM)
    dma = pltpu.SemaphoreType.DMA
    return pl.pallas_call(
        functools.partial(kernel, ngx, ngy),
        out_shape=jax.ShapeDtypeStruct((5, cx, cy, nz), f32),
        in_specs=[hbm, hbm, hbm, vmem, vmem, vmem, hbm],
        out_specs=vmem,
        scratch_shapes=[
            pltpu.VMEM((5, cx + 4, cy, nz), f32),
            pltpu.VMEM((5, cx, cy + 8, nz), f32),
            pltpu.VMEM((2, 5, cx, 2, nz), f32),
            pltpu.VMEM((2, 5, cx, 2, nz), f32),
            pltpu.VMEM((cx, cy, nz), jnp.int32),
            pltpu.VMEM((ngy, cap, nbr, nbr), f32),
            pltpu.VMEM((5, cx + 1, cy, nz), f32),
            pltpu.VMEM((5, cx * cy, 2 * nz), bf16),
            pltpu.VMEM((total, LANES), jnp.int32),
            pltpu.VMEM((total, LANES), jnp.int32),
            pltpu.VMEM((ngy, cx * cy, entries), bf16),
            pltpu.VMEM((ngy, nz, entries), bf16),
            pltpu.VMEM((total, 2 * LANES, LANES), bf16),
            pltpu.VMEM((ngy, 5, entries), f32),
            pltpu.VMEM((ngy, 5, entries), f32),
            pltpu.VMEM((ngy, 5, entries), f32),
            pltpu.VMEM((ngy, 5, entries), f32),
            dma((5,)), dma((4,)), dma((4,)),
            dma((ngy,)), dma((ngy,)), dma((ngy,)), dma((ngy,)),
        ],
        compiler_params=pltpu.CompilerParams(
            collective_id=0, has_side_effects=True, vmem_limit_bytes=48 * 1024 * 1024
        ),
        name="euler_section",
    )(dens_pres, velocity, cut_class, nbhd_cells, helper_list, live_counts, redist_weights)


def solution(mesh):
    in_specs = (
        P(None, "gx", "gy", None),
        P(None, "gx", "gy", None),
        P("gx", "gy", None),
        P("gx", "gy", None, None),
        P("gx", "gy", None),
        P("gx", "gy"),
        P("gx", "gy", None, None, None, None),
    )
    out_specs = P(None, "gx", "gy", None)
    body = functools.partial(local, mesh.shape["gx"], mesh.shape["gy"])
    return jax.shard_map(body, mesh=mesh, in_specs=in_specs, out_specs=out_specs, check_vma=False)
```

```python
import functools

import jax
import jax.numpy as jnp
from jax import lax
from jax.experimental import pallas as pl
from jax.experimental.pallas import tpu as pltpu
from jax.sharding import PartitionSpec as P

GAS_GAMMA = 1.4
STEP_RATIO = 0.3
MESH = pl.DeviceIdType.MESH
NT = (((1,), (1,)), ((), ()))
LANES = 128


def minmod(a, b):
    return jnp.maximum(jnp.minimum(a, b), 0.0) + jnp.minimum(jnp.maximum(a, b), 0.0)


def conserved(q):
    rho, u, v, w, p = q
    energy = p * (1.0 / (GAS_GAMMA - 1.0)) + 0.5 * rho * (u * u + v * v + w * w)
    return [rho, rho * u, rho * v, rho * w, energy]


def state_flux(q, normal):
    rho, p, un = q[0], q[4], q[1 + normal]
    cons = conserved(q)
    flux = [part * un for part in cons]
    flux[1 + normal] = flux[1 + normal] + p
    flux[4] = flux[4] + p * un
    gp = GAS_GAMMA * p
    return cons, flux, jnp.abs(un) + gp * lax.rsqrt(gp * rho)


def double_flux(lower, upper, normal):
    cl, fl, sl = state_flux(lower, normal)
    cu, fu, su = state_flux(upper, normal)
    wave = jnp.maximum(sl, su)
    return [a + b - wave * (d - c) for a, b, c, d in zip(fl, fu, cl, cu)]


def cyclic_divergence(q, normal, axis):
    size = q[0].shape[axis]
    before = lambda t: pltpu.roll(t, 1, axis)
    after = lambda t: pltpu.roll(t, size - 1, axis)
    jumps = [t - before(t) for t in q]
    halves = [0.5 * minmod(j, after(j)) for j in jumps]
    lower = [t + s for t, s in zip(q, halves)]
    upper = [after(t - s) for t, s in zip(q, halves)]
    flux = double_flux(lower, upper, normal)
    return [f - before(f) for f in flux]


def split2(t):
    high = t.astype(jnp.bfloat16)
    return high, (t - high.astype(jnp.float32)).astype(jnp.bfloat16)


def kernel(ngx, ngy, dp_ref, vel_ref, cut_ref, cells_ref, help_ref, live_ref, w_ref, out_ref,
           px, py, ysend, yrecv, cutv, cellv, helpv, livev, wv, acc, dmat, ridx, zidx, ohr, ohz, wbd,
           sendv, arrived, mixed, returned,
           lsem, hsend, hrecv, asend, arecv, bsend, brecv):
    gx = lax.axis_index("gx")
    gy = lax.axis_index("gy")
    _, cx, cy, nz = dp_ref.shape
    cap, nbr = w_ref.shape[3], w_ref.shape[4]
    slots = cells_ref.shape[2]
    pack = LANES // nbr
    rows = cap // pack
    entries = cap * nbr
    cells_xy = cx * cy

    loads = [
        pltpu.make_async_copy(dp_ref.at[0], px.at[0, pl.ds(2, cx)], lsem.at[0]),
        pltpu.make_async_copy(dp_ref.at[1], px.at[4, pl.ds(2, cx)], lsem.at[1]),
        pltpu.make_async_copy(vel_ref, px.at[pl.ds(1, 3), pl.ds(2, cx)], lsem.at[2]),
    ]
    later = [
        pltpu.make_async_copy(w_ref.at[0, 0], wv, lsem.at[3]),
        pltpu.make_async_copy(cut_ref, cutv, lsem.at[4]),
    ]
    tables = [
        pltpu.make_async_copy(cells_ref, cellv, lsem.at[5]),
        pltpu.make_async_copy(help_ref, helpv, lsem.at[6]),
        pltpu.make_async_copy(live_ref, livev, lsem.at[7]),
    ]
    for copy in loads + tables + later:
        copy.start()

    xlo = {"gx": lax.rem(gx + ngx - 1, ngx)}
    xhi = {"gx": lax.rem(gx + 1, ngx)}
    ylo = {"gy": lax.rem(gy + ngy - 1, ngy)}
    yhi = {"gy": lax.rem(gy + 1, ngy)}
    barrier = pltpu.get_barrier_semaphore()
    for target in (xlo, xhi):
        pl.semaphore_signal(barrier, inc=1, device_id=target, device_id_type=MESH)
    for k in range(1, ngy):
        pl.semaphore_signal(barrier, inc=1, device_id={"gy": lax.rem(gy + k, ngy)}, device_id_type=MESH)

    for copy in loads:
        copy.wait()

    def fill_rows(x, carry):
        for v in range(5):
            q = px[v, x + 2]
            py[v, x, pl.ds(0, cy), :] = q
            ysend[0, v, x] = q[0:2]
            ysend[1, v, x] = q[cy - 2:cy]
        return carry

    lax.fori_loop(0, cx, fill_rows, 0)
    pl.semaphore_wait(barrier, ngy + 1)

    def remote(src, dst, send, recv, target):
        return pltpu.make_async_remote_copy(src_ref=src, dst_ref=dst, send_sem=send, recv_sem=recv,
                                            device_id=target, device_id_type=MESH)

    halos = [
        remote(px.at[:, pl.ds(2, 2)], px.at[:, pl.ds(cx + 2, 2)], hsend.at[0], hrecv.at[0], xlo),
        remote(px.at[:, pl.ds(cx, 2)], px.at[:, pl.ds(0, 2)], hsend.at[1], hrecv.at[1], xhi),
        remote(ysend.at[0], yrecv.at[1], hsend.at[2], hrecv.at[2], ylo),
        remote(ysend.at[1], yrecv.at[0], hsend.at[3], hrecv.at[3], yhi),
    ]
    for copy in halos:
        copy.start()

    for copy in tables:
        copy.wait()
    names = helpv[0].astype(jnp.float32)
    sub = lax.broadcasted_iota(jnp.int32, (slots, slots), 0)
    lane = lax.broadcasted_iota(jnp.int32, (slots, slots), 1)
    spread = jnp.broadcast_to(names, (slots, slots))
    column = jnp.sum(jnp.where(sub == lane, spread, 0.0), axis=1, keepdims=True)
    ranks = jnp.sum(jnp.where((column == spread) & (sub < lane), 1.0, 0.0), axis=0, keepdims=True)
    place = names * float(cap) + ranks
    live = lax.broadcasted_iota(jnp.int32, (1, slots), 1) < livev[...]
    place = jnp.where(live, place, -1.0)
    cells = cellv[0, 0]
    shift = nz.bit_length() - 1
    cell_row = ((cells >> shift) + 1).astype(jnp.float32).astype(jnp.bfloat16)
    cell_z = ((cells & (nz - 1)) + 1).astype(jnp.float32).astype(jnp.bfloat16)
    total = ngy * rows
    target_row = lax.broadcasted_iota(jnp.int32, (total, slots), 0) * pack
    parts_r, parts_z = [], []
    for j in range(pack):
        hot = jnp.where((target_row + j).astype(jnp.float32) == place, 1.0, 0.0).astype(jnp.bfloat16)
        parts_r.append(jnp.dot(hot, cell_row, preferred_element_type=jnp.float32))
        parts_z.append(jnp.dot(hot, cell_z, preferred_element_type=jnp.float32))
    ridx[...] = jnp.concatenate(parts_r, axis=1).astype(jnp.int32) - 1
    zidx[...] = jnp.concatenate(parts_z, axis=1).astype(jnp.int32) - 1

    def lane_row(ref, h):
        return jnp.concatenate([ref[pl.ds(h * rows + i, 1), :] for i in range(rows)], axis=1)

    def one_hots(h, carry):
        z_of = lane_row(zidx, h)
        ohz[h] = jnp.where(lax.broadcasted_iota(jnp.int32, (nz, entries), 0) == z_of, 1.0, 0.0).astype(jnp.bfloat16)
        return carry

    lax.fori_loop(0, ngy, one_hots, 0)

    def z_part(x, carry):
        for v, t in enumerate(cyclic_divergence([px[v, x + 2] for v in range(5)], 2, 1)):
            acc[v, x + 1] = t
        return carry

    lax.fori_loop(0, cx, z_part, 0)

    for copy in later:
        copy.wait()

    halos[0].wait_recv()
    halos[1].wait_recv()

    jump0 = [px[v, 1] - px[v, 0] for v in range(5)]
    jump1 = [px[v, 2] - px[v, 1] for v in range(5)]
    low0 = [px[v, 1] + 0.5 * minmod(jump0[v], jump1[v]) for v in range(5)]

    def x_part(f, carry):
        lower, jump, before = carry
        here = [px[v, f + 2] for v in range(5)]
        ahead = [px[v, f + 3] - here[v] for v in range(5)]
        halves = [0.5 * minmod(a, b) for a, b in zip(jump, ahead)]
        flux = double_flux(lower, [t - s for t, s in zip(here, halves)], 0)
        for v in range(5):
            acc[v, f] += flux[v] - before[v]
        return [t + s for t, s in zip(here, halves)], ahead, flux

    for v in range(5):
        acc[v, 0] = jnp.zeros((cy, nz), jnp.float32)
    lax.fori_loop(0, cx + 1, x_part, (low0, jump1, [jnp.zeros((cy, nz), jnp.float32)] * 5))

    halos[2].wait_recv()
    halos[3].wait_recv()

    def y_part(x, carry):
        for v in range(5):
            py[v, x, pl.ds(cy, 2), :] = yrecv[1, v, x]
            py[v, x, pl.ds(cy + 2, 2), :] = yrecv[1, v, x]
            py[v, x, pl.ds(cy + 4, 2), :] = yrecv[0, v, x]
            py[v, x, pl.ds(cy + 6, 2), :] = yrecv[0, v, x]
        q = [py[v, x] for v in range(5)]
        div = cyclic_divergence(q, 1, 0)
        scale = (-2.0 * STEP_RATIO) / (1.0 + cutv[x].astype(jnp.float32))
        cons = conserved([t[0:cy] for t in q])
        for v in range(5):
            delta = (acc[v, x + 1] + div[v][0:cy]) * scale
            out_ref[v, x] = cons[v] + delta
            high, low = split2(delta)
            start = pl.multiple_of(x * cy, cy)
            dmat[v, pl.ds(start, cy), pl.ds(0, nz)] = high
            dmat[v, pl.ds(start, cy), pl.ds(nz, nz)] = low
        return carry

    lax.fori_loop(0, cx, y_part, 0)

    def gather(k, h):
        hot_z = ohz[h]
        stacked = jnp.concatenate([hot_z, hot_z], axis=0)
        mask = lax.broadcasted_iota(jnp.int32, (cells_xy, entries), 0) == lane_row(ridx, h)
        for v in range(5):
            picked = jnp.dot(dmat[v], stacked, preferred_element_type=jnp.float32)
            line = jnp.sum(jnp.where(mask, picked, 0.0), axis=0, keepdims=True)
            for i in range(rows):
                sendv[k, pl.ds(i * 5 + v, 1), :] = line[:, i * LANES:(i + 1) * LANES]

    def mix(source, k, dest):
        b = lax.rem(gy + ngy - k, ngy)
        for i in range(rows):
            high, low = split2(source[k, pl.ds(i * 5, 5), :])
            w = wbd[b * rows + i]
            first = lax.dot_general(high, w, NT, preferred_element_type=jnp.float32)
            second = lax.dot_general(low, w[0:LANES], NT, preferred_element_type=jnp.float32)
            dest[k, pl.ds(i * 5, 5), :] = first[:, 0:LANES] + first[:, LANES:] + second

    def scatter(k):
        h = lax.rem(gy + k, ngy)
        change = returned[k] - sendv[k]
        hot_r = ohr[h]
        hot_z = ohz[h]
        for v in range(5):
            line = jnp.concatenate([change[i * 5 + v:i * 5 + v + 1] for i in range(rows)], axis=1)
            high, low = split2(line)
            moved = lax.dot_general(hot_r * high, hot_z, NT, preferred_element_type=jnp.float32)
            moved += lax.dot_general(hot_r * low, hot_z, NT, preferred_element_type=jnp.float32)
            out_ref[v] += moved.reshape(cx, cy, nz)

    out_copies, back_copies = [None], [None]
    for k in range(1, ngy):
        target = {"gy": lax.rem(gy + k, ngy)}
        gather(k, lax.rem(gy + k, ngy))
        copy = remote(sendv.at[k], arrived.at[k], asend.at[k], arecv.at[k], target)
        copy.start()
        out_copies.append(copy)
    def weights(t, carry):
        b = t // rows
        i = t % rows
        for part in range(2):
            for j in range(pack):
                high, low = split2(wv[b, i * pack + j])
                piece = high if part == 0 else low
                blank = jnp.zeros((nbr, nbr), jnp.bfloat16)
                full = jnp.concatenate([blank] * j + [piece] + [blank] * (pack - 1 - j), axis=1)
                wbd[t, pl.ds(part * LANES + j * nbr, nbr), :] = full
        return carry

    lax.fori_loop(0, total, weights, 0)

    gather(0, gy)
    mix(sendv, 0, returned)
    for k in range(1, ngy):
        out_copies[k].wait_recv()
        mix(arrived, k, mixed)
        source = {"gy": lax.rem(gy + ngy - k, ngy)}
        copy = remote(mixed.at[k], returned.at[k], bsend.at[k], brecv.at[k], source)
        copy.start()
        back_copies.append(copy)
    def row_hots(h, carry):
        r_of = lane_row(ridx, h)
        ohr[h] = jnp.where(lax.broadcasted_iota(jnp.int32, (cells_xy, entries), 0) == r_of, 1.0, 0.0).astype(jnp.bfloat16)
        return carry

    lax.fori_loop(0, ngy, row_hots, 0)

    scatter(0)
    for k in range(1, ngy):
        back_copies[k].wait_recv()
        scatter(k)
    for copy in halos + out_copies[1:] + back_copies[1:]:
        copy.wait_send()


def local(ngx, ngy, dens_pres, velocity, cut_class, nbhd_cells, helper_list, live_counts, redist_weights):
    _, cx, cy, nz = dens_pres.shape
    cap, nbr = redist_weights.shape[3:5]
    pack = LANES // nbr
    rows = cap // pack
    total = ngy * rows
    entries = cap * nbr
    f32, bf16 = jnp.float32, jnp.bfloat16
    hbm = pl.BlockSpec(memory_space=pltpu.HBM)
    vmem = pl.BlockSpec(memory_space=pltpu.VMEM)
    dma = pltpu.SemaphoreType.DMA
    return pl.pallas_call(
        functools.partial(kernel, ngx, ngy),
        out_shape=jax.ShapeDtypeStruct((5, cx, cy, nz), f32),
        in_specs=[hbm] * 7,
        out_specs=vmem,
        scratch_shapes=[
            pltpu.VMEM((5, cx + 4, cy, nz), f32),
            pltpu.VMEM((5, cx, cy + 8, nz), f32),
            pltpu.VMEM((2, 5, cx, 2, nz), f32),
            pltpu.VMEM((2, 5, cx, 2, nz), f32),
            pltpu.VMEM((cx, cy, nz), jnp.int32),
            pltpu.VMEM(nbhd_cells.shape, jnp.int32),
            pltpu.VMEM(helper_list.shape, jnp.int32),
            pltpu.VMEM(live_counts.shape, jnp.int32),
            pltpu.VMEM((ngy, cap, nbr, nbr), f32),
            pltpu.VMEM((5, cx + 1, cy, nz), f32),
            pltpu.VMEM((5, cx * cy, 2 * nz), bf16),
            pltpu.VMEM((total, LANES), jnp.int32),
            pltpu.VMEM((total, LANES), jnp.int32),
            pltpu.VMEM((ngy, cx * cy, entries), bf16),
            pltpu.VMEM((ngy, nz, entries), bf16),
            pltpu.VMEM((total, 2 * LANES, LANES), bf16),
            pltpu.VMEM((ngy, 5 * rows, LANES), f32),
            pltpu.VMEM((ngy, 5 * rows, LANES), f32),
            pltpu.VMEM((ngy, 5 * rows, LANES), f32),
            pltpu.VMEM((ngy, 5 * rows, LANES), f32),
            dma((8,)), dma((4,)), dma((4,)),
            dma((ngy,)), dma((ngy,)), dma((ngy,)), dma((ngy,)),
        ],
        compiler_params=pltpu.CompilerParams(
            collective_id=0, has_side_effects=True, vmem_limit_bytes=63 * 1024 * 1024
        ),
        name="euler_section",
    )(dens_pres, velocity, cut_class, nbhd_cells, helper_list, live_counts, redist_weights)


def solution(mesh):
    in_specs = (
        P(None, "gx", "gy", None),
        P(None, "gx", "gy", None),
        P("gx", "gy", None),
        P("gx", "gy", None, None),
        P("gx", "gy", None),
        P("gx", "gy"),
        P("gx", "gy", None, None, None, None),
    )
    out_specs = P(None, "gx", "gy", None)
    body = functools.partial(local, mesh.shape["gx"], mesh.shape["gy"])
    return jax.shard_map(body, mesh=mesh, in_specs=in_specs, out_specs=out_specs, check_vma=False)
```
